512 devices in a mesh: expert: 8 (over z_hi, core), dp: 64 (over z_lo, y, x).
Axes of the slice: x: 4, y: 8, z: 8 (z_hi: 4, z_lo: 2; z = z_hi * 2 + z_lo), core: 2. Of those that a mesh axis runs over, the one named last changes fastest.
Arguments:
- hidden: bfloat16 [8, 1024, 8192], P('expert', None, 'dp'), may hold values from -0.1875 to 0.1875
- out_grad: bfloat16 [8, 1024, 6144], P('expert', 'dp'), may hold values from -16 to 16
- gate_weight: float32 [8, 1024], P('expert'), may hold values from 0.1 to 1
- counts: int32 [8], P('expert'), may hold values from 512 to 1024
- carried_error: bfloat16 [8, 8192, 6144], P('expert', 'dp'), may hold values from -40 to 40
- old_query: float32 [6144, 32], P('dp'), may hold values from -6 to 6
Outputs:
- new_error: bfloat16 [8, 8192, 6144], P('expert', 'dp')
- new_query: float32 [6144, 32], P('dp')
The draws below stay inside these ranges and needn't reach their ends.
Inputs may be any that keep to these rules, and one draw needn't show every extreme that they name: In every draw at least one replica has all its slots live.
All inputs are finite; a program needn't handle non-finite values.
Results may differ from the reference program's by a relative error of at most 0.0034.
Values may be sent and summed in bfloat16 or wider, within the bound.
No kernel may reach another device: no remote copies, remote signals or barrier semaphores. Data moves between devices by JAX's collectives and lax.ppermute only.
A program may use at most 64 MiB of HBM per device.

```python
import jax
import jax.numpy as jnp
from jax import lax

D = 6144
FF = 8192
RANK = 32
SLOTS = 1024
REPLICAS = 8


def draw_counts(key, part):
    key = jax.random.fold_in(key, 11)
    first_key, second_key = jax.random.split(key)
    drawn = jax.random.randint(first_key, (REPLICAS,), SLOTS // 2, SLOTS + 1)
    full_replica = jax.random.randint(second_key, (), 0, REPLICAS)
    return jnp.where(jnp.arange(REPLICAS) == full_replica, SLOTS, drawn).astype(jnp.int32)


def draw_carried_error(key, part):
    key = jax.random.fold_in(key, 23)
    row_key = jax.random.fold_in(key, 0)
    column_key = jax.random.fold_in(key, 1)
    own_key = jax.random.fold_in(key, 3)
    rising = 3.0 ** (jnp.arange(FF, dtype=jnp.float32) / FF - 0.5)
    row_spread = 10.0 ** (jax.random.uniform(row_key, (REPLICAS, FF, 1)) - 0.5)
    column_spread = 10.0 ** (jax.random.uniform(column_key, (REPLICAS, 1, D)) - 0.5)
    base = jnp.clip(jax.random.normal(own_key, (REPLICAS, FF, D)), -4.0, 4.0)
    return (0.5 * base * rising[None, :, None] * row_spread * column_spread).astype(jnp.bfloat16)


def raised(entries, key, source, target, shards_of, factor):
    owner, partner = [(jnp.arange(entries.shape[position]) // (entries.shape[position] // shards_of)).reshape([-1 if axis == position else 1 for axis in range(entries.ndim)]) for position in (source, target)]
    chosen = jax.random.permutation(key, shards_of)[partner]
    strong = (owner == chosen) | (owner == (partner + shards_of // 2) % shards_of)
    return jnp.where(strong, factor * entries, entries)


def level_of(stream_key, extent, pieces, low, top_value):
    level = 1.0
    for dim, shards_of in pieces:
        heights = jax.random.uniform(jax.random.fold_in(jax.random.fold_in(stream_key, 6), dim), (shards_of,), jnp.float32, low / len(pieces), top_value / len(pieces))
        level = level * jnp.repeat(jnp.exp(heights), extent[dim] // shards_of).reshape((-1,) + (1,) * (len(extent) - 1 - dim))
    return level


def centred(stream_key, dims, width, most, cuts=(), kind=jnp.bfloat16):
    level = level_of(stream_key, dims, cuts, -0.22, 0.18) if cuts else 1.0
    values = jax.random.normal(stream_key, dims, jnp.float32) * width * level
    return jnp.minimum(jnp.maximum(values, -most), most).astype(kind)


def noise_with(key, shape, scale, limit, shards, heavy, kind=jnp.bfloat16):
    values = scale * jax.random.normal(key, shape, jnp.float32)
    if shards:
        values = values * level_of(key, shape, shards, -0.22, 0.18)
    return jnp.clip(raised(values, jax.random.fold_in(key, 3), *heavy), -limit, limit).astype(kind)


def setup_inputs(seed: int = 0) -> dict:
    keys = jax.random.split(jax.random.key(seed), 7)
    return {
        "hidden": centred(keys[0], (REPLICAS, SLOTS, FF), SLOTS ** -0.5, 0.1875, ((0, 8), (2, 64))),
        "out_grad": noise_with(keys[1], (REPLICAS, SLOTS, D), 1.0, 16.0, ((0, 8), (1, 64)), (1, 2, 64, 4.0)),
        "gate_weight": jnp.clip(0.1 + 0.9 * jax.random.uniform(keys[2], (REPLICAS, SLOTS), jnp.float32) ** level_of(keys[2], (REPLICAS, SLOTS), ((0, 8),), -0.2, 0.2), 0.1, 1.0),
        "counts": draw_counts(jax.random.fold_in(keys[6], 71), 0),
        "carried_error": draw_carried_error(jax.random.fold_in(keys[6], 71), 0),
        "old_query": centred(keys[5], (D, RANK), 1.0, 6.0, ((0, 64),), jnp.float32),
    }


exact_mode = lax.Precision.HIGHEST

def right_solve(chol_lower, values):
    return lax.linalg.triangular_solve(chol_lower, values, left_side=False, lower=True, transpose_a=True)

def contract_rows(left_side, right_side):
    return lax.dot_general(left_side.astype(jnp.float32), right_side.astype(jnp.float32), (((0,), (0,)), ((), ())), precision=exact_mode, preferred_element_type=jnp.float32)

def reference(hidden, out_grad, gate_weight, counts, carried_error, old_query):
    slot_ids = lax.iota(jnp.int32, SLOTS)
    live_slots = slot_ids[None, :] < counts[:, None]
    slot_scale = jnp.where(live_slots, gate_weight, jnp.zeros_like(gate_weight))
    weighted = (hidden.astype(jnp.float32) * slot_scale[:, :, None]).astype(jnp.bfloat16)
    query_low = old_query.astype(jnp.bfloat16)
    query_wide = lax.optimization_barrier(query_low).astype(jnp.float32)
    members = (weighted, out_grad, carried_error)

    def left_term(member):
        weight_rows, grad_rows, error_rows = member
        slot_query = jnp.dot(grad_rows.astype(jnp.float32), query_low.astype(jnp.float32), preferred_element_type=jnp.float32)
        return contract_rows(weight_rows.astype(jnp.float32), slot_query) + jnp.dot(error_rows.astype(jnp.float32), query_wide, precision=exact_mode)
    left_sum = jnp.sum(lax.map(left_term, members), axis=0) / REPLICAS
    gram_matrix = jnp.dot(left_sum.T, left_sum, precision=exact_mode)
    chol_lower = jnp.linalg.cholesky(gram_matrix)
    left_basis = right_solve(chol_lower, left_sum)

    def query_term(member):
        weight_rows, grad_rows, error_rows = member
        slot_vectors = jnp.dot(weight_rows.astype(jnp.float32), left_basis, precision=exact_mode)
        return contract_rows(grad_rows.astype(jnp.float32), slot_vectors) + contract_rows(error_rows.astype(jnp.float32), left_basis)
    new_query = jnp.sum(lax.map(query_term, members), axis=0) / REPLICAS
    correction = jnp.dot(left_basis, new_query.T, precision=exact_mode)

    def error_term(member):
        weight_rows, grad_rows, error_rows = member
        local_grad = lax.dot_general(weight_rows.astype(jnp.float32), grad_rows.astype(jnp.float32), (((0,), (0,)), ((), ())), preferred_element_type=jnp.float32)
        return (local_grad + error_rows.astype(jnp.float32) - correction).astype(jnp.bfloat16)
    new_error = lax.map(error_term, members)
    return (new_error, new_query)
```

```python
import jax
import jax.numpy as jnp
from jax import lax
from jax.sharding import Mesh, PartitionSpec as P

EXPERT = ("zh", "core")
DP = ("zl", "y", "x")
PLANE = ("y", "x")
exact_mode = lax.Precision.HIGHEST
f32 = jnp.float32
bf16 = jnp.bfloat16


def exchange(blocks, axes):
    return lax.all_to_all(blocks, axes, split_axis=0, concat_axis=0, tiled=True)


def spread(block, axes, count):
    return exchange(jnp.broadcast_to(block[None], (count,) + block.shape), axes)


def halves(values):
    high = lax.reduce_precision(values, 8, 7)
    return high.astype(bf16), (values - high).astype(bf16)


def product(left_side, right_side, left_dim, right_dim):
    return lax.dot_general(
        left_side,
        right_side,
        (((left_dim,), (right_dim,)), ((), ())),
        preferred_element_type=f32,
    )


def body(hidden, out_grad, gate_weight, counts, carried_error, old_query):
    hidden_local = hidden[0]
    grad_rows = out_grad[0]
    error_local = carried_error[0]
    slots, units = hidden_local.shape
    own_slots, width = grad_rows.shape
    own_rows, rank = old_query.shape
    replicas = lax.axis_size(EXPERT)
    members = lax.axis_size(DP)
    plane = lax.axis_size(PLANE)
    pair = lax.axis_size("zl")

    query_low = old_query.astype(bf16)
    query_blocks = spread(query_low.T, DP, members)
    full_query = query_blocks.transpose(1, 0, 2).reshape(rank, width)

    pair_rows = lax.all_gather(grad_rows, "zl", axis=0, tiled=True)
    full_grad = lax.all_gather(pair_rows, PLANE, axis=0, tiled=True)

    live_slots = lax.iota(jnp.int32, slots) < counts[0]
    slot_scale = jnp.where(live_slots, gate_weight[0], jnp.zeros_like(gate_weight[0]))
    weighted = (hidden_local.astype(f32) * slot_scale[:, None]).astype(bf16)

    slot_query = product(grad_rows, full_query, 1, 1)
    all_slots = spread(slot_query, DP, members).reshape(slots, rank)
    slot_pair = jnp.concatenate(halves(all_slots), axis=1)
    left_pair = product(weighted, slot_pair, 0, 0)
    left_part = left_pair[:, :rank] + left_pair[:, rank:] + product(error_local, full_query, 1, 1)
    left_sum = jnp.sum(spread(left_part, EXPERT, replicas), axis=0) / replicas

    sum_pair = jnp.concatenate(halves(left_sum), axis=1)
    slot_parts = product(weighted, sum_pair, 1, 0)
    slot_parts = slot_parts[:, :rank] + slot_parts[:, rank:]
    gram_part = lax.dot_general(
        left_sum, left_sum, (((0,), (0,)), ((), ())), precision=exact_mode, preferred_element_type=f32
    )
    outgoing = jnp.concatenate(
        [
            slot_parts.reshape(members, own_slots, rank),
            jnp.broadcast_to(gram_part[None], (members, rank, rank)),
        ],
        axis=1,
    )
    summed = jnp.sum(exchange(outgoing, DP), axis=0)
    own_vectors = summed[:own_slots]
    gram_matrix = summed[own_slots:]

    vector_pair = jnp.concatenate(halves(own_vectors), axis=1)
    query_pair = product(vector_pair, grad_rows, 0, 0) + product(sum_pair, error_local, 0, 0)
    query_part = query_pair[:rank] + query_pair[rank:]
    query_part = query_part.reshape(rank, members, own_rows).transpose(1, 0, 2)
    own_part = jnp.sum(exchange(query_part, DP), axis=0)
    own_sum = jnp.sum(spread(own_part, EXPERT, replicas), axis=0) / replicas

    chol_lower = jnp.linalg.cholesky(gram_matrix)
    inverse = lax.linalg.triangular_solve(
        chol_lower, jnp.eye(rank, dtype=f32), left_side=True, lower=True
    )
    left_basis = lax.dot_general(
        left_sum, inverse, (((1,), (1,)), ((), ())), precision=exact_mode, preferred_element_type=f32
    )
    new_cols = jnp.dot(inverse, own_sum, precision=exact_mode, preferred_element_type=f32)
    new_rows = new_cols.T
    all_cols = spread(new_cols, DP, members).transpose(1, 0, 2).reshape(rank, width)

    basis_high, basis_low = halves(left_basis)
    cols_high, cols_low = halves(all_cols)
    correction = product(
        jnp.concatenate([basis_high, basis_low, basis_high], axis=1),
        jnp.concatenate([cols_high, cols_high, cols_low], axis=0),
        1,
        0,
    )
    ordered = weighted.reshape(pair, plane, own_slots, units).transpose(1, 0, 2, 3).reshape(slots, units)
    local_grad = product(ordered, full_grad, 0, 0)
    new_error = (local_grad + error_local.astype(f32) - correction).astype(bf16)
    return (new_error[None], new_rows)


def solution(mesh):
    fine = Mesh(mesh.devices.reshape(4, 2, 2, 8, 4), EXPERT + DP)
    in_specs = (
        P(EXPERT, None, DP),
        P(EXPERT, DP, None),
        P(EXPERT, None),
        P(EXPERT),
        P(EXPERT, DP, None),
        P(DP, None),
    )
    out_specs = (P(EXPERT, DP, None), P(DP, None))
    return jax.shard_map(body, mesh=fine, in_specs=in_specs, out_specs=out_specs, check_vma=False)
```

```python
import jax
import jax.numpy as jnp
from jax import lax
from jax.sharding import Mesh, PartitionSpec as P

EXPERT = ("zh", "core")
DP = ("zl", "y", "x")
PLANE = ("y", "x")
exact_mode = lax.Precision.HIGHEST
f32 = jnp.float32
bf16 = jnp.bfloat16


def exchange(blocks, axes):
    return lax.all_to_all(blocks, axes, split_axis=0, concat_axis=0, tiled=True)


def spread(block, axes, count):
    return exchange(jnp.broadcast_to(block[None], (count,) + block.shape), axes)


def halves(values):
    high = lax.reduce_precision(values, 8, 7)
    return high.astype(bf16), (values - high).astype(bf16)


def product(left_side, right_side, left_dim, right_dim):
    return lax.dot_general(
        left_side,
        right_side,
        (((left_dim,), (right_dim,)), ((), ())),
        preferred_element_type=f32,
    )


def body(hidden, out_grad, gate_weight, counts, carried_error, old_query):
    hidden_local = hidden[0]
    grad_rows = out_grad[0]
    error_local = carried_error[0]
    slots, units = hidden_local.shape
    own_slots, width = grad_rows.shape
    own_rows, rank = old_query.shape
    replicas = lax.axis_size(EXPERT)
    members = lax.axis_size(DP)
    plane = lax.axis_size(PLANE)

    query_low = old_query.astype(bf16)
    query_blocks = spread(query_low.T, DP, members)
    partner_rows = lax.ppermute(grad_rows, "zl", [(0, 1), (1, 0)])
    pair_rows = jnp.concatenate([grad_rows, partner_rows], axis=0)
    query_blocks, pair_rows = lax.optimization_barrier((query_blocks, pair_rows))
    full_grad = lax.all_gather(pair_rows, PLANE, axis=0, tiled=True)
    full_query = query_blocks.transpose(1, 0, 2).reshape(rank, width)

    live_slots = lax.iota(jnp.int32, slots) < counts[0]
    slot_scale = jnp.where(live_slots, gate_weight[0], jnp.zeros_like(gate_weight[0]))
    weighted = (hidden_local.astype(f32) * slot_scale[:, None]).astype(bf16)

    slot_query = product(grad_rows, full_query, 1, 1)
    slot_pair = spread(jnp.concatenate(halves(slot_query), axis=1), DP, members).reshape(slots, 2 * rank)
    left_pair = product(weighted, slot_pair, 0, 0)
    left_part = left_pair[:, :rank] + left_pair[:, rank:] + product(error_local, full_query, 1, 1)
    left_sum = jnp.sum(spread(left_part, EXPERT, replicas), axis=0) / replicas

    sum_high, sum_low = halves(left_sum)
    slot_parts = product(
        jnp.concatenate([weighted, weighted], axis=1), jnp.concatenate([sum_high, sum_low], axis=0), 1, 0
    )
    gram_part = lax.dot_general(
        left_sum, left_sum, (((0,), (0,)), ((), ())), precision=exact_mode, preferred_element_type=f32
    )
    gram_wide = jnp.concatenate([gram_part[:own_slots], gram_part[own_slots:]], axis=1)
    outgoing = jnp.concatenate(
        [
            slot_parts.reshape(members, own_slots, rank),
            jnp.broadcast_to(gram_wide[None], (members,) + gram_wide.shape),
        ],
        axis=2,
    )
    summed = jnp.sum(exchange(outgoing, DP), axis=0)
    own_vectors = summed[:, :rank]
    gram_matrix = jnp.concatenate([summed[:, rank : 2 * rank], summed[:, 2 * rank :]], axis=0)

    sum_pair = jnp.concatenate([sum_high, sum_low], axis=1)
    vector_pair = jnp.concatenate(halves(own_vectors), axis=1)
    query_pair = product(vector_pair, grad_rows, 0, 0) + product(sum_pair, error_local, 0, 0)
    query_part = query_pair[:rank] + query_pair[rank:]
    query_part = query_part.reshape(rank, members, own_rows).transpose(1, 0, 2)
    own_part = jnp.sum(exchange(query_part, DP), axis=0)
    own_sum = jnp.sum(spread(own_part, EXPERT, replicas), axis=0) / replicas

    chol_lower = jnp.linalg.cholesky(gram_matrix)
    inverse = lax.linalg.triangular_solve(
        chol_lower, jnp.eye(rank, dtype=f32), left_side=True, lower=True
    )
    left_basis = lax.dot_general(
        left_sum, inverse, (((1,), (1,)), ((), ())), precision=exact_mode, preferred_element_type=f32
    )
    new_cols = jnp.dot(inverse, own_sum, precision=exact_mode, preferred_element_type=f32)
    new_rows = new_cols.T
    col_blocks = spread(jnp.concatenate(halves(new_cols), axis=0), DP, members)

    own_first = lax.axis_index("zl") == 0
    parts = weighted.reshape(2, plane, own_slots, units)
    ordered = jnp.where(
        own_first,
        jnp.stack([parts[0], parts[1]], axis=1),
        jnp.stack([parts[1], parts[0]], axis=1),
    ).reshape(slots, units)
    merged = product(ordered, full_grad, 0, 0) + error_local.astype(f32)
    merged, col_blocks = lax.optimization_barrier((merged, col_blocks))
    col_pair = col_blocks.transpose(1, 0, 2).reshape(2 * rank, width)
    basis_high, basis_low = halves(left_basis)
    correction = product(
        jnp.concatenate([basis_high, basis_high], axis=1), col_pair, 1, 0
    ) + product(basis_low, col_pair[:rank], 1, 0)
    new_error = (merged - correction).astype(bf16)
    return (new_error[None], new_rows)


def solution(mesh):
    fine = Mesh(mesh.devices.reshape(4, 2, 2, 8, 4), EXPERT + DP)
    in_specs = (
        P(EXPERT, None, DP),
        P(EXPERT, DP, None),
        P(EXPERT, None),
        P(EXPERT),
        P(EXPERT, DP, None),
        P(DP, None),
    )
    out_specs = (P(EXPERT, DP, None), P(DP, None))
    return jax.shard_map(body, mesh=fine, in_specs=in_specs, out_specs=out_specs, check_vma=False)
```

```python
import jax
import jax.numpy as jnp
from jax import lax
from jax.sharding import Mesh, PartitionSpec as P

EXPERT = ("zh", "core")
DP = ("zl", "y", "x")
PLANE = ("y", "x")
exact_mode = lax.Precision.HIGHEST
f32 = jnp.float32
bf16 = jnp.bfloat16


def exchange(blocks, axes):
    return lax.all_to_all(blocks, axes, split_axis=0, concat_axis=0, tiled=True)


def spread(block, axes, count):
    return exchange(jnp.broadcast_to(block[None], (count,) + block.shape), axes)


def swap(values):
    return lax.ppermute(values, "zl", [(0, 1), (1, 0)])


def halves(values):
    high = lax.reduce_precision(values, 8, 7)
    return high.astype(bf16), (values - high).astype(bf16)


def product(left_side, right_side, left_dim, right_dim):
    return lax.dot_general(
        left_side,
        right_side,
        (((left_dim,), (right_dim,)), ((), ())),
        preferred_element_type=f32,
    )


def body(hidden, out_grad, gate_weight, counts, carried_error, old_query):
    hidden_local = hidden[0]
    grad_rows = out_grad[0]
    error_local = carried_error[0]
    slots, units = hidden_local.shape
    own_slots, width = grad_rows.shape
    own_rows, rank = old_query.shape
    replicas = lax.axis_size(EXPERT)
    members = lax.axis_size(DP)
    plane = lax.axis_size(PLANE)

    query_low = old_query.astype(bf16)
    query_blocks = spread(query_low.T, DP, members)
    live_slots = lax.iota(jnp.int32, slots) < counts[0]
    slot_scale = jnp.where(live_slots, gate_weight[0], jnp.zeros_like(gate_weight[0]))
    weighted = (hidden_local.astype(f32) * slot_scale[:, None]).astype(bf16)

    own_first = lax.axis_index("zl") == 0
    half = width // 2
    left_cols, right_cols = grad_rows[:, :half], grad_rows[:, half:]
    kept_rows = jnp.where(own_first, left_cols, right_cols)
    partner_rows = swap(jnp.where(own_first, right_cols, left_cols))
    pair_rows = jnp.concatenate([kept_rows, partner_rows], axis=0)
    query_blocks, pair_rows = lax.optimization_barrier((query_blocks, pair_rows))
    half_grad = lax.all_gather(pair_rows, PLANE, axis=0, tiled=True)
    pair_weighted = jnp.concatenate([weighted, swap(weighted)], axis=1)
    full_query = query_blocks.transpose(1, 0, 2).reshape(rank, width)

    slot_query = product(grad_rows, full_query, 1, 1)
    slot_high, slot_low = halves(slot_query)
    slot_wide = jnp.concatenate([slot_high, slot_low, jnp.zeros((own_slots, 2 * rank), bf16)], axis=1)
    all_slots = spread(slot_wide, DP, members).reshape(slots, 4 * rank)
    left_pair = product(weighted, all_slots, 0, 0)
    left_part = left_pair[:, :rank] + left_pair[:, rank : 2 * rank] + product(error_local, full_query, 1, 1)
    left_sum = jnp.sum(spread(left_part, EXPERT, replicas), axis=0) / replicas

    sum_high, sum_low = halves(left_sum)
    slot_parts = product(
        jnp.concatenate([weighted, weighted], axis=1), jnp.concatenate([sum_high, sum_low], axis=0), 1, 0
    )
    gram_part = lax.dot_general(
        left_sum, left_sum, (((0,), (0,)), ((), ())), precision=exact_mode, preferred_element_type=f32
    )
    gram_wide = jnp.concatenate([gram_part[:own_slots], gram_part[own_slots:]], axis=1)
    outgoing = jnp.concatenate(
        [
            slot_parts.reshape(members, own_slots, rank),
            jnp.broadcast_to(gram_wide[None], (members,) + gram_wide.shape),
        ],
        axis=2,
    )
    summed = jnp.sum(exchange(outgoing, DP), axis=0)
    own_vectors = summed[:, :rank]
    gram_matrix = jnp.concatenate([summed[:, rank : 2 * rank], summed[:, 2 * rank :]], axis=0)

    sum_pair = jnp.concatenate([sum_high, sum_low], axis=1)
    vector_pair = jnp.concatenate(halves(own_vectors), axis=1)
    query_pair = product(vector_pair, grad_rows, 0, 0) + product(sum_pair, error_local, 0, 0)
    query_part = query_pair[:rank] + query_pair[rank:]
    query_part = query_part.reshape(rank, members, own_rows).transpose(1, 0, 2)
    own_part = jnp.sum(exchange(query_part, DP), axis=0)
    own_sum = jnp.sum(spread(own_part, EXPERT, replicas), axis=0) / replicas

    chol_lower = jnp.linalg.cholesky(gram_matrix)
    inverse = lax.linalg.triangular_solve(
        chol_lower, jnp.eye(rank, dtype=f32), left_side=True, lower=True
    )
    left_basis = lax.dot_general(
        left_sum, inverse, (((1,), (1,)), ((), ())), precision=exact_mode, preferred_element_type=f32
    )
    new_cols = jnp.dot(inverse, own_sum, precision=exact_mode, preferred_element_type=f32)
    new_rows = new_cols.T
    col_blocks = spread(jnp.concatenate(halves(new_cols), axis=0), DP, members)

    parts = pair_weighted.reshape(2, plane, own_slots, 2 * units)
    ordered = jnp.where(
        own_first,
        jnp.stack([parts[0], parts[1]], axis=1),
        jnp.stack([parts[1], parts[0]], axis=1),
    ).reshape(slots, 2 * units)
    both_grad = product(ordered, half_grad, 0, 0)
    kept_grad, sent_grad = both_grad[:units], swap(both_grad[units:])
    merged = (
        jnp.concatenate(
            [
                jnp.where(own_first, kept_grad, sent_grad),
                jnp.where(own_first, sent_grad, kept_grad),
            ],
            axis=1,
        )
        + error_local.astype(f32)
    )
    merged, col_blocks = lax.optimization_barrier((merged, col_blocks))
    col_pair = col_blocks.transpose(1, 0, 2).reshape(2 * rank, width)
    basis_high, basis_low = halves(left_basis)
    correction = product(
        jnp.concatenate([basis_high, basis_high], axis=1), col_pair, 1, 0
    ) + product(jnp.concatenate([basis_low, jnp.zeros_like(basis_low)], axis=1), col_pair, 1, 0)
    new_error = (merged - correction).astype(bf16)
    return (new_error[None], new_rows)


def solution(mesh):
    fine = Mesh(mesh.devices.reshape(4, 2, 2, 8, 4), EXPERT + DP)
    in_specs = (
        P(EXPERT, None, DP),
        P(EXPERT, DP, None),
        P(EXPERT, None),
        P(EXPERT),
        P(EXPERT, DP, None),
        P(DP, None),
    )
    out_specs = (P(EXPERT, DP, None), P(DP, None))
    return jax.shard_map(body, mesh=fine, in_specs=in_specs, out_specs=out_specs, check_vma=False)
```

```python
import jax
import jax.numpy as jnp
from jax import lax
from jax.sharding import Mesh, PartitionSpec as P

EXPERT = ("zh", "core")
DP = ("zl", "y", "x")
PLANE = ("y", "x")
exact_mode = lax.Precision.HIGHEST
f32 = jnp.float32
bf16 = jnp.bfloat16


def exchange(blocks, axes):
    return lax.all_to_all(blocks, axes, split_axis=0, concat_axis=0, tiled=True)


def spread(block, axes, count):
    return exchange(jnp.broadcast_to(block[None], (count,) + block.shape), axes)


def swap(values):
    return lax.ppermute(values, "zl", [(0, 1), (1, 0)])


def swap_core(values):
    return lax.ppermute(values, "core", [(0, 1), (1, 0)])


def halves(values):
    high = lax.reduce_precision(values, 8, 7)
    return high.astype(bf16), (values - high).astype(bf16)


def product(left_side, right_side, left_dim, right_dim):
    return lax.dot_general(
        left_side,
        right_side,
        (((left_dim,), (right_dim,)), ((), ())),
        preferred_element_type=f32,
    )


def body(hidden, out_grad, gate_weight, counts, carried_error, old_query):
    hidden_local = hidden[0]
    grad_rows = out_grad[0]
    error_local = carried_error[0]
    slots, units = hidden_local.shape
    own_slots, width = grad_rows.shape
    own_rows, rank = old_query.shape
    replicas = lax.axis_size(EXPERT)
    members = lax.axis_size(DP)

    query_low = old_query.astype(bf16)
    query_blocks = spread(query_low.T, DP, members)
    live_slots = lax.iota(jnp.int32, slots) < counts[0]
    slot_scale = jnp.where(live_slots, gate_weight[0], jnp.zeros_like(gate_weight[0]))
    weighted = (hidden_local.astype(f32) * slot_scale[:, None]).astype(bf16)

    pair_rows = jnp.concatenate([grad_rows, swap(grad_rows)], axis=0)
    full_grad = lax.all_gather(pair_rows, PLANE, axis=0, tiled=True)
    full_query = query_blocks.transpose(1, 0, 2).reshape(rank, width)

    slot_query = product(grad_rows, full_query, 1, 1)
    slot_high, slot_low = halves(slot_query)
    slot_wide = jnp.concatenate([slot_high, slot_low, jnp.zeros((own_slots, 2 * rank), bf16)], axis=1)
    all_slots = spread(slot_wide, DP, members).reshape(slots, 4 * rank)
    left_pair = product(weighted, all_slots, 0, 0)
    left_part = left_pair[:, :rank] + left_pair[:, rank : 2 * rank] + product(error_local, full_query, 1, 1)
    left_sum = jnp.sum(spread(left_part, EXPERT, replicas), axis=0) / replicas

    sum_high, sum_low = halves(left_sum)
    slot_parts = product(
        jnp.concatenate([weighted, weighted], axis=1), jnp.concatenate([sum_high, sum_low], axis=0), 1, 0
    )
    gram_part = lax.dot_general(
        left_sum, left_sum, (((0,), (0,)), ((), ())), precision=exact_mode, preferred_element_type=f32
    )
    gram_wide = jnp.concatenate([gram_part[:own_slots], gram_part[own_slots:]], axis=1)
    outgoing = jnp.concatenate(
        [
            slot_parts.reshape(members, own_slots, rank),
            jnp.broadcast_to(gram_wide[None], (members,) + gram_wide.shape),
        ],
        axis=2,
    )
    summed = jnp.sum(exchange(outgoing, DP), axis=0)
    own_vectors = summed[:, :rank]
    gram_matrix = jnp.concatenate([summed[:, rank : 2 * rank], summed[:, 2 * rank :]], axis=0)

    sum_pair = jnp.concatenate([sum_high, sum_low], axis=1)
    vector_pair = jnp.concatenate(halves(own_vectors), axis=1)
    query_pair = product(vector_pair, grad_rows, 0, 0) + product(sum_pair, error_local, 0, 0)
    query_part = query_pair[:rank] + query_pair[rank:]
    first_core = lax.axis_index("core") == 0
    upper, lower = query_part[: rank // 2], query_part[rank // 2 :]
    core_part = jnp.where(first_core, upper, lower) + swap_core(jnp.where(first_core, lower, upper))
    core_part = core_part.reshape(rank // 2, members, own_rows).transpose(1, 0, 2)
    incoming = exchange(core_part, DP)
    own_part = jnp.sum(incoming, axis=0)
    expert_parts = spread(own_part, EXPERT, replicas)
    own_sum = jnp.sum(expert_parts.reshape(-1, rank, own_rows), axis=0) / replicas

    chol_lower = jnp.linalg.cholesky(gram_matrix)
    inverse = lax.linalg.triangular_solve(
        chol_lower, jnp.eye(rank, dtype=f32), left_side=True, lower=True
    )
    left_basis = lax.dot_general(
        left_sum, inverse, (((1,), (1,)), ((), ())), precision=exact_mode, preferred_element_type=f32
    )
    new_cols = jnp.dot(inverse, own_sum, precision=exact_mode, preferred_element_type=f32)
    new_rows = new_cols.T
    cols_high, cols_low = halves(new_cols)
    half_rank = rank // 2
    sent_cols = jnp.where(
        first_core,
        jnp.concatenate([cols_high[:half_rank], cols_low[:half_rank]], axis=0),
        jnp.concatenate([cols_high[half_rank:], cols_low[half_rank:]], axis=0),
    )
    col_blocks = spread(sent_cols, DP, members)

    own_first = lax.axis_index("zl") == 0
    parts = weighted.reshape(2, lax.axis_size(PLANE), own_slots, units)
    ordered = jnp.stack(
        [jnp.where(own_first, parts[0], parts[1]), jnp.where(own_first, parts[1], parts[0])], axis=1
    ).reshape(slots, units)
    merged = product(ordered, full_grad, 0, 0) + error_local.astype(f32)
    merged, col_blocks = lax.optimization_barrier((merged, col_blocks))
    core_cols = col_blocks.transpose(1, 0, 2).reshape(rank, width)
    all_cols = jnp.concatenate([core_cols, swap_core(core_cols)], axis=0)
    left_half, right_half = left_basis[:, :half_rank], left_basis[:, half_rank:]
    own_high, own_low = halves(jnp.where(first_core, left_half, right_half))
    other_high, other_low = halves(jnp.where(first_core, right_half, left_half))
    nothing = jnp.zeros_like(own_low)
    correction = product(
        jnp.concatenate([own_high, own_high, other_high, other_high], axis=1), all_cols, 1, 0
    ) + product(jnp.concatenate([own_low, nothing, other_low, nothing], axis=1), all_cols, 1, 0)
    new_error = (merged - correction).astype(bf16)
    return (new_error[None], new_rows)


def solution(mesh):
    fine = Mesh(mesh.devices.reshape(4, 2, 2, 8, 4), EXPERT + DP)
    in_specs = (
        P(EXPERT, None, DP),
        P(EXPERT, DP, None),
        P(EXPERT, None),
        P(EXPERT),
        P(EXPERT, DP, None),
        P(DP, None),
    )
    out_specs = (P(EXPERT, DP, None), P(DP, None))
    return jax.shard_map(body, mesh=fine, in_specs=in_specs, out_specs=out_specs, check_vma=False)
```

```python
import jax
import jax.numpy as jnp
from jax import lax
from jax.sharding import Mesh, PartitionSpec as P

EXPERT = ("zh", "core")
DP = ("zl", "y", "x")
PLANE = ("y", "x")
exact_mode = lax.Precision.HIGHEST
f32 = jnp.float32
bf16 = jnp.bfloat16


def exchange(blocks, axes):
    return lax.all_to_all(blocks, axes, split_axis=0, concat_axis=0, tiled=True)


def spread(block, axes, count):
    return exchange(jnp.broadcast_to(block[None], (count,) + block.shape), axes)


def swap(values):
    return lax.ppermute(values, "zl", [(0, 1), (1, 0)])


def swap_core(values):
    return lax.ppermute(values, "core", [(0, 1), (1, 0)])


def fold(blocks):
    middle = blocks.shape[1] // 2
    return jnp.concatenate([blocks[:, :middle], blocks[:, middle:]], axis=2)


def unfold(values):
    middle = values.shape[1] // 2
    return jnp.concatenate([values[:, :middle], values[:, middle:]], axis=0)


def halves(values):
    high = lax.reduce_precision(values, 8, 7)
    return high.astype(bf16), (values - high).astype(bf16)


def product(left_side, right_side, left_dim, right_dim):
    return lax.dot_general(
        left_side,
        right_side,
        (((left_dim,), (right_dim,)), ((), ())),
        preferred_element_type=f32,
    )


def body(hidden, out_grad, gate_weight, counts, carried_error, old_query):
    hidden_local = hidden[0]
    grad_rows = out_grad[0]
    error_local = carried_error[0]
    slots, units = hidden_local.shape
    own_slots, width = grad_rows.shape
    own_rows, rank = old_query.shape
    replicas = lax.axis_size(EXPERT)
    members = lax.axis_size(DP)

    query_low = old_query.astype(bf16)
    query_blocks = spread(query_low.T, DP, members)
    live_slots = lax.iota(jnp.int32, slots) < counts[0]
    slot_scale = jnp.where(live_slots, gate_weight[0], jnp.zeros_like(gate_weight[0]))
    weighted = (hidden_local.astype(f32) * slot_scale[:, None]).astype(bf16)

    pair_rows = jnp.concatenate([grad_rows, swap(grad_rows)], axis=0)
    query_blocks, pair_rows = lax.optimization_barrier((query_blocks, pair_rows))
    full_grad = lax.all_gather(pair_rows, PLANE, axis=0, tiled=True)
    full_query = query_blocks.transpose(1, 0, 2).reshape(rank, width)

    slot_query = product(grad_rows, full_query, 1, 1)
    slot_high, slot_low = halves(slot_query)
    slot_wide = jnp.concatenate([slot_high, slot_low, jnp.zeros((own_slots, 2 * rank), bf16)], axis=1)
    all_slots = spread(slot_wide, DP, members).reshape(slots, 4 * rank)
    left_pair = product(weighted, all_slots, 0, 0)
    left_part = left_pair[:, :rank] + left_pair[:, rank : 2 * rank] + product(error_local, full_query, 1, 1)
    left_sum = jnp.sum(spread(left_part, EXPERT, replicas), axis=0) / replicas

    sum_high, sum_low = halves(left_sum)
    slot_parts = product(
        jnp.concatenate([weighted, weighted], axis=1), jnp.concatenate([sum_high, sum_low], axis=0), 1, 0
    )
    gram_part = lax.dot_general(
        left_sum, left_sum, (((0,), (0,)), ((), ())), precision=exact_mode, preferred_element_type=f32
    )
    first_core = lax.axis_index("core") == 0
    half_rank = rank // 2
    gram_half = jnp.where(first_core, gram_part[:half_rank], gram_part[half_rank:])
    outgoing = jnp.concatenate(
        [
            fold(slot_parts.reshape(members, own_slots, rank)),
            jnp.broadcast_to(fold(gram_half[None]), (members, half_rank // 2, 2 * rank)),
        ],
        axis=2,
    )
    summed = jnp.sum(exchange(outgoing, DP), axis=0)
    own_vectors = unfold(summed[:, : 2 * rank])
    gram_half = unfold(summed[:, 2 * rank :])
    other_half = swap_core(gram_half)
    gram_matrix = jnp.concatenate(
        [jnp.where(first_core, gram_half, other_half), jnp.where(first_core, other_half, gram_half)], axis=0
    )

    sum_pair = jnp.concatenate([sum_high, sum_low], axis=1)
    vector_pair = jnp.concatenate(halves(own_vectors), axis=1)
    query_pair = product(vector_pair, grad_rows, 0, 0) + product(sum_pair, error_local, 0, 0)
    query_part = query_pair[:rank] + query_pair[rank:]
    upper, lower = query_part[: rank // 2], query_part[rank // 2 :]
    core_part = jnp.where(first_core, upper, lower) + swap_core(jnp.where(first_core, lower, upper))
    core_part = core_part.reshape(rank // 2, members, own_rows).transpose(1, 0, 2)
    incoming = exchange(core_part, DP)
    own_part = jnp.sum(incoming, axis=0)
    expert_parts = spread(own_part, EXPERT, replicas)
    own_sum = jnp.sum(expert_parts.reshape(-1, rank, own_rows), axis=0) / replicas

    chol_lower = jnp.linalg.cholesky(gram_matrix)
    inverse = lax.linalg.triangular_solve(
        chol_lower, jnp.eye(rank, dtype=f32), left_side=True, lower=True
    )
    left_basis = lax.dot_general(
        left_sum, inverse, (((1,), (1,)), ((), ())), precision=exact_mode, preferred_element_type=f32
    )
    new_cols = jnp.dot(inverse, own_sum, precision=exact_mode, preferred_element_type=f32)
    new_rows = new_cols.T
    cols_high, cols_low = halves(new_cols)
    sent_cols = jnp.where(
        first_core,
        jnp.concatenate([cols_high[:half_rank], cols_low[:half_rank]], axis=0),
        jnp.concatenate([cols_high[half_rank:], cols_low[half_rank:]], axis=0),
    )
    col_blocks = spread(sent_cols, DP, members)

    own_first = lax.axis_index("zl") == 0
    parts = weighted.reshape(2, lax.axis_size(PLANE), own_slots, units)
    ordered = jnp.stack(
        [jnp.where(own_first, parts[0], parts[1]), jnp.where(own_first, parts[1], parts[0])], axis=1
    ).reshape(slots, units)
    merged = product(ordered, full_grad, 0, 0) + error_local.astype(f32)
    merged, col_blocks = lax.optimization_barrier((merged, col_blocks))
    core_cols = col_blocks.transpose(1, 0, 2).reshape(rank, width)
    all_cols = jnp.concatenate([core_cols, swap_core(core_cols)], axis=0)
    left_half, right_half = left_basis[:, :half_rank], left_basis[:, half_rank:]
    own_high, own_low = halves(jnp.where(first_core, left_half, right_half))
    other_high, other_low = halves(jnp.where(first_core, right_half, left_half))
    nothing = jnp.zeros_like(own_low)
    correction = product(
        jnp.concatenate([own_high, own_high, other_high, other_high], axis=1), all_cols, 1, 0
    ) + product(jnp.concatenate([own_low, nothing, other_low, nothing], axis=1), all_cols, 1, 0)
    new_error = (merged - correction).astype(bf16)
    return (new_error[None], new_rows)


def solution(mesh):
    fine = Mesh(mesh.devices.reshape(4, 2, 2, 8, 4), EXPERT + DP)
    in_specs = (
        P(EXPERT, None, DP),
        P(EXPERT, DP, None),
        P(EXPERT, None),
        P(EXPERT),
        P(EXPERT, DP, None),
        P(DP, None),
    )
    out_specs = (P(EXPERT, DP, None), P(DP, None))
    return jax.shard_map(body, mesh=fine, in_specs=in_specs, out_specs=out_specs, check_vma=False)
```

```python
import jax
import jax.numpy as jnp
from jax import lax
from jax.sharding import Mesh, PartitionSpec as P

EXPERT = ("zh", "core")
DP = ("zl", "y", "x")
PLANE = ("y", "x")
exact_mode = lax.Precision.HIGHEST
f32 = jnp.float32
bf16 = jnp.bfloat16


def exchange(blocks, axes):
    return lax.all_to_all(blocks, axes, split_axis=0, concat_axis=0, tiled=True)


def spread(block, axes, count):
    return exchange(jnp.broadcast_to(block[None], (count,) + block.shape), axes)


def swap(values):
    return lax.ppermute(values, "zl", [(0, 1), (1, 0)])


def swap_core(values):
    return lax.ppermute(values, "core", [(0, 1), (1, 0)])


def fold(blocks):
    middle = blocks.shape[1] // 2
    return jnp.concatenate([blocks[:, :middle], blocks[:, middle:]], axis=2)


def unfold(values):
    middle = values.shape[1] // 2
    return jnp.concatenate([values[:, :middle], values[:, middle:]], axis=0)


def halves(values):
    high = lax.reduce_precision(values, 8, 7)
    return high.astype(bf16), (values - high).astype(bf16)


def product(left_side, right_side, left_dim, right_dim):
    return lax.dot_general(
        left_side,
        right_side,
        (((left_dim,), (right_dim,)), ((), ())),
        preferred_element_type=f32,
    )


def body(hidden, out_grad, gate_weight, counts, carried_error, old_query):
    hidden_local = hidden[0]
    grad_rows = out_grad[0]
    error_local = carried_error[0]
    slots, units = hidden_local.shape
    own_slots, width = grad_rows.shape
    own_rows, rank = old_query.shape
    replicas = lax.axis_size(EXPERT)
    members = lax.axis_size(DP)

    query_low = old_query.astype(bf16)
    query_blocks = spread(query_low.T, DP, members)
    live_slots = lax.iota(jnp.int32, slots) < counts[0]
    slot_scale = jnp.where(live_slots, gate_weight[0], jnp.zeros_like(gate_weight[0]))
    weighted = (hidden_local.astype(f32) * slot_scale[:, None]).astype(bf16)

    pair_rows = jnp.concatenate([grad_rows, swap(grad_rows)], axis=0)
    full_grad = lax.all_gather(pair_rows, PLANE, axis=0, tiled=True)
    full_query = query_blocks.transpose(1, 0, 2).reshape(rank, width)

    slot_query = product(grad_rows, full_query, 1, 1)
    slot_high, slot_low = halves(slot_query)
    slot_wide = jnp.concatenate([slot_high, slot_low, jnp.zeros((own_slots, 2 * rank), bf16)], axis=1)
    all_slots = spread(slot_wide, DP, members).reshape(slots, 4 * rank)
    left_pair = product(weighted, all_slots, 0, 0)
    left_part = left_pair[:, :rank] + left_pair[:, rank : 2 * rank] + product(error_local, full_query, 1, 1)
    left_sum = jnp.sum(spread(left_part, EXPERT, replicas), axis=0) / replicas

    sum_high, sum_low = halves(left_sum)
    slot_parts = product(
        jnp.concatenate([weighted, weighted], axis=1), jnp.concatenate([sum_high, sum_low], axis=0), 1, 0
    )
    gram_part = lax.dot_general(
        left_sum, left_sum, (((0,), (0,)), ((), ())), precision=exact_mode, preferred_element_type=f32
    )
    first_core = lax.axis_index("core") == 0
    half_rank = rank // 2
    gram_half = jnp.where(first_core, gram_part[:half_rank], gram_part[half_rank:])
    outgoing = jnp.concatenate(
        [
            fold(slot_parts.reshape(members, own_slots, rank)),
            jnp.broadcast_to(fold(gram_half[None]), (members, half_rank // 2, 2 * rank)),
        ],
        axis=2,
    )
    summed = jnp.sum(exchange(outgoing, DP), axis=0)
    own_vectors = unfold(summed[:, : 2 * rank])
    gram_half = unfold(summed[:, 2 * rank :])
    other_half = swap_core(gram_half)
    gram_matrix = jnp.concatenate(
        [jnp.where(first_core, gram_half, other_half), jnp.where(first_core, other_half, gram_half)], axis=0
    )

    sum_pair = jnp.concatenate([sum_high, sum_low], axis=1)
    vector_pair = jnp.concatenate(halves(own_vectors), axis=1)
    query_pair = product(vector_pair, grad_rows, 0, 0) + product(sum_pair, error_local, 0, 0)
    query_part = query_pair[:rank] + query_pair[rank:]
    upper, lower = query_part[: rank // 2], query_part[rank // 2 :]
    core_part = jnp.where(first_core, upper, lower) + swap_core(jnp.where(first_core, lower, upper))
    core_part = core_part.reshape(rank // 2, members, own_rows).transpose(1, 0, 2)
    incoming = exchange(core_part, DP)
    own_part = jnp.sum(incoming, axis=0)
    expert_parts = spread(own_part, EXPERT, replicas)
    own_sum = jnp.sum(expert_parts.reshape(-1, rank, own_rows), axis=0) / replicas

    chol_lower = jnp.linalg.cholesky(gram_matrix)
    inverse = lax.linalg.triangular_solve(
        chol_lower, jnp.eye(rank, dtype=f32), left_side=True, lower=True
    )
    left_basis = lax.dot_general(
        left_sum, inverse, (((1,), (1,)), ((), ())), precision=exact_mode, preferred_element_type=f32
    )
    new_cols = jnp.dot(inverse, own_sum, precision=exact_mode, preferred_element_type=f32)
    new_rows = new_cols.T
    cols_high, cols_low = halves(new_cols)
    sent_cols = jnp.where(
        first_core,
        jnp.concatenate([cols_high[:half_rank], cols_low[:half_rank]], axis=0),
        jnp.concatenate([cols_high[half_rank:], cols_low[half_rank:]], axis=0),
    )
    col_blocks = spread(sent_cols, DP, members)

    own_first = lax.axis_index("zl") == 0
    parts = weighted.reshape(2, lax.axis_size(PLANE), own_slots, units)
    ordered = jnp.stack(
        [jnp.where(own_first, parts[0], parts[1]), jnp.where(own_first, parts[1], parts[0])], axis=1
    ).reshape(slots, units)
    merged = product(ordered, full_grad, 0, 0) + error_local.astype(f32)
    merged, col_blocks = lax.optimization_barrier((merged, col_blocks))
    core_cols = col_blocks.transpose(1, 0, 2).reshape(rank, width)
    all_cols = jnp.concatenate([core_cols, swap_core(core_cols)], axis=0)
    left_half, right_half = left_basis[:, :half_rank], left_basis[:, half_rank:]
    own_high, own_low = halves(jnp.where(first_core, left_half, right_half))
    other_high, other_low = halves(jnp.where(first_core, right_half, left_half))
    nothing = jnp.zeros_like(own_low)
    correction = product(
        jnp.concatenate([own_high, own_high, other_high, other_high], axis=1), all_cols, 1, 0
    ) + product(jnp.concatenate([own_low, nothing, other_low, nothing], axis=1), all_cols, 1, 0)
    new_error = (merged - correction).astype(bf16)
    return (new_error[None], new_rows)


def solution(mesh):
    fine = Mesh(mesh.devices.reshape(4, 2, 2, 8, 4), EXPERT + DP)
    in_specs = (
        P(EXPERT, None, DP),
        P(EXPERT, DP, None),
        P(EXPERT, None),
        P(EXPERT),
        P(EXPERT, DP, None),
        P(DP, None),
    )
    out_specs = (P(EXPERT, DP, None), P(DP, None))
    return jax.shard_map(body, mesh=fine, in_specs=in_specs, out_specs=out_specs, check_vma=False)
```

```python
import jax
import jax.numpy as jnp
from jax import lax
from jax.sharding import Mesh, PartitionSpec as P

EXPERT = ("zh", "core")
DP = ("zl", "y", "x")
PLANE = ("y", "x")
exact_mode = lax.Precision.HIGHEST
f32 = jnp.float32
bf16 = jnp.bfloat16


def exchange(blocks, axes):
    return lax.all_to_all(blocks, axes, split_axis=0, concat_axis=0, tiled=True)


def spread(block, axes, count):
    return exchange(jnp.broadcast_to(block[None], (count,) + block.shape), axes)


def swap(values):
    return lax.ppermute(values, "zl", [(0, 1), (1, 0)])


def swap_core(values):
    return lax.ppermute(values, "core", [(0, 1), (1, 0)])


def arrange(values, own_first):
    slots, units = values.shape
    plane = lax.axis_size(PLANE)
    parts = values.reshape(2, plane, slots // (2 * plane), units)
    return jnp.stack(
        [jnp.where(own_first, parts[0], parts[1]), jnp.where(own_first, parts[1], parts[0])], axis=1
    ).reshape(slots, units)


def fold(blocks):
    middle = blocks.shape[1] // 2
    return jnp.concatenate([blocks[:, :middle], blocks[:, middle:]], axis=2)


def unfold(values):
    middle = values.shape[1] // 2
    return jnp.concatenate([values[:, :middle], values[:, middle:]], axis=0)


def halves(values):
    high = lax.reduce_precision(values, 8, 7)
    return high.astype(bf16), (values - high).astype(bf16)


def product(left_side, right_side, left_dim, right_dim):
    return lax.dot_general(
        left_side,
        right_side,
        (((left_dim,), (right_dim,)), ((), ())),
        preferred_element_type=f32,
    )


def body(hidden, out_grad, gate_weight, counts, carried_error, old_query):
    hidden_local = hidden[0]
    grad_rows = out_grad[0]
    error_local = carried_error[0]
    slots, units = hidden_local.shape
    own_slots, width = grad_rows.shape
    own_rows, rank = old_query.shape
    replicas = lax.axis_size(EXPERT)
    members = lax.axis_size(DP)

    query_low = old_query.astype(bf16)
    query_blocks = spread(query_low.T, DP, members)
    live_slots = lax.iota(jnp.int32, slots) < counts[0]
    slot_scale = jnp.where(live_slots, gate_weight[0], jnp.zeros_like(gate_weight[0]))
    weighted = (hidden_local.astype(f32) * slot_scale[:, None]).astype(bf16)

    own_first = lax.axis_index("zl") == 0
    half = width // 2
    left_cols, right_cols = grad_rows[:, :half], grad_rows[:, half:]
    kept_rows = jnp.where(own_first, left_cols, right_cols)
    pair_rows = jnp.concatenate(
        [kept_rows, swap(jnp.where(own_first, right_cols, left_cols))], axis=0
    )
    query_blocks, pair_rows = lax.optimization_barrier((query_blocks, pair_rows))
    half_grad = lax.all_gather(pair_rows, PLANE, axis=0, tiled=True)
    partner_weighted = swap(weighted)
    full_query = query_blocks.transpose(1, 0, 2).reshape(rank, width)

    slot_query = product(grad_rows, full_query, 1, 1)
    slot_high, slot_low = halves(slot_query)
    slot_wide = jnp.concatenate([slot_high, slot_low, jnp.zeros((own_slots, 2 * rank), bf16)], axis=1)
    all_slots = spread(slot_wide, DP, members).reshape(slots, 4 * rank)
    left_pair = product(weighted, all_slots, 0, 0)
    left_part = left_pair[:, :rank] + left_pair[:, rank : 2 * rank] + product(error_local, full_query, 1, 1)
    left_sum = jnp.sum(spread(left_part, EXPERT, replicas), axis=0) / replicas

    sum_high, sum_low = halves(left_sum)
    slot_parts = product(
        jnp.concatenate([weighted, weighted], axis=1), jnp.concatenate([sum_high, sum_low], axis=0), 1, 0
    )
    gram_part = lax.dot_general(
        left_sum, left_sum, (((0,), (0,)), ((), ())), precision=exact_mode, preferred_element_type=f32
    )
    first_core = lax.axis_index("core") == 0
    half_rank = rank // 2
    gram_half = jnp.where(first_core, gram_part[:half_rank], gram_part[half_rank:])
    outgoing = jnp.concatenate(
        [
            fold(slot_parts.reshape(members, own_slots, rank)),
            jnp.broadcast_to(fold(gram_half[None]), (members, half_rank // 2, 2 * rank)),
        ],
        axis=2,
    )
    summed = jnp.sum(exchange(outgoing, DP), axis=0)
    own_vectors = unfold(summed[:, : 2 * rank])
    gram_half = unfold(summed[:, 2 * rank :])
    other_half = swap_core(gram_half)
    gram_matrix = jnp.concatenate(
        [jnp.where(first_core, gram_half, other_half), jnp.where(first_core, other_half, gram_half)], axis=0
    )

    sum_pair = jnp.concatenate([sum_high, sum_low], axis=1)
    vector_pair = jnp.concatenate(halves(own_vectors), axis=1)
    query_pair = product(vector_pair, grad_rows, 0, 0) + product(sum_pair, error_local, 0, 0)
    query_part = query_pair[:rank] + query_pair[rank:]
    upper, lower = query_part[: rank // 2], query_part[rank // 2 :]
    core_part = jnp.where(first_core, upper, lower) + swap_core(jnp.where(first_core, lower, upper))
    core_part = core_part.reshape(rank // 2, members, own_rows).transpose(1, 0, 2)
    incoming = exchange(core_part, DP)
    own_part = jnp.sum(incoming, axis=0)
    expert_parts = spread(own_part, EXPERT, replicas)
    sent_grad = product(arrange(partner_weighted, own_first), half_grad, 0, 0).astype(bf16)
    expert_parts, sent_grad = lax.optimization_barrier((expert_parts, sent_grad))
    partner_grad = swap(sent_grad).astype(f32)
    own_sum = jnp.sum(expert_parts.reshape(-1, rank, own_rows), axis=0) / replicas

    chol_lower = jnp.linalg.cholesky(gram_matrix)
    inverse = lax.linalg.triangular_solve(
        chol_lower, jnp.eye(rank, dtype=f32), left_side=True, lower=True
    )
    left_basis = lax.dot_general(
        left_sum, inverse, (((1,), (1,)), ((), ())), precision=exact_mode, preferred_element_type=f32
    )
    new_cols = jnp.dot(inverse, own_sum, precision=exact_mode, preferred_element_type=f32)
    new_rows = new_cols.T
    cols_high, cols_low = halves(new_cols)
    sent_cols = jnp.where(
        first_core,
        jnp.concatenate([cols_high[:half_rank], cols_low[:half_rank]], axis=0),
        jnp.concatenate([cols_high[half_rank:], cols_low[half_rank:]], axis=0),
    )
    col_blocks = spread(sent_cols, DP, members)

    kept_grad = product(arrange(weighted, own_first), half_grad, 0, 0)
    merged = (
        jnp.concatenate(
            [
                jnp.where(own_first, kept_grad, partner_grad),
                jnp.where(own_first, partner_grad, kept_grad),
            ],
            axis=1,
        )
        + error_local.astype(f32)
    )
    merged, col_blocks = lax.optimization_barrier((merged, col_blocks))
    core_cols = col_blocks.transpose(1, 0, 2).reshape(rank, width)
    all_cols = jnp.concatenate([core_cols, swap_core(core_cols)], axis=0)
    left_half, right_half = left_basis[:, :half_rank], left_basis[:, half_rank:]
    own_high, own_low = halves(jnp.where(first_core, left_half, right_half))
    other_high, other_low = halves(jnp.where(first_core, right_half, left_half))
    nothing = jnp.zeros_like(own_low)
    correction = product(
        jnp.concatenate([own_high, own_high, other_high, other_high], axis=1), all_cols, 1, 0
    ) + product(jnp.concatenate([own_low, nothing, other_low, nothing], axis=1), all_cols, 1, 0)
    new_error = (merged - correction).astype(bf16)
    return (new_error[None], new_rows)


def solution(mesh):
    fine = Mesh(mesh.devices.reshape(4, 2, 2, 8, 4), EXPERT + DP)
    in_specs = (
        P(EXPERT, None, DP),
        P(EXPERT, DP, None),
        P(EXPERT, None),
        P(EXPERT),
        P(EXPERT, DP, None),
        P(DP, None),
    )
    out_specs = (P(EXPERT, DP, None), P(DP, None))
    return jax.shard_map(body, mesh=fine, in_specs=in_specs, out_specs=out_specs, check_vma=False)
```
